128 devices in a mesh: blk: 32 (over x, z, y_lo), dp: 4 (over y_hi, core).
Axes of the slice: x: 4, y: 4 (y_hi: 2, y_lo: 2; y = y_hi * 2 + y_lo), z: 4, core: 2. Of those that a mesh axis runs over, the one named last changes fastest.
Arguments:
- embeddings: bfloat16 [32768, 512], P(('dp', 'blk')), may hold values from -16 to 16
- centers: bfloat16 [65536, 512], P(('blk', 'dp')), may hold values from -10 to 10
- labels: int32 [32768], P(('dp', 'blk')), may hold values from 0 to 65535
Outputs:
- loss: float32 [32768], P(('dp', 'blk'))
The draws below stay inside these ranges and needn't reach their ends.
All inputs are finite; a program needn't handle non-finite values.
Results may differ from the reference program's by a relative error of at most 0.0017.
Values may be sent and summed in bfloat16 or wider, within the bound.
No kernel may reach another device: no remote copies, remote signals or barrier semaphores. Data moves between devices by JAX's collectives and lax.ppermute only.
A program may use at most 128 MiB of HBM per device.

```python
import math
import jax
import jax.numpy as jnp
from jax import lax

D = 512
BATCH = 32768
CLASSES = 65536


def label_values(key):
    return jax.random.randint(jax.random.fold_in(key, 11), (BATCH,), 0, CLASSES, dtype=jnp.int32)


def center_values(key):
    center_key = jax.random.fold_in(key, 12)
    return jax.random.truncated_normal(center_key, -6.0, 6.0, (CLASSES, D), jnp.float32)


def draw_labels(key, part):
    return label_values(key)


def draw_centers(key, part):
    return center_values(key).astype(jnp.bfloat16)


def draw_embeddings(key, part):
    labels = label_values(key)
    centers = center_values(key).astype(jnp.bfloat16).astype(jnp.float32)
    unit = centers * jax.lax.rsqrt(jnp.sum(centers * centers, axis=1, keepdims=True) + 1e-06)
    negatives = jax.random.randint(jax.random.fold_in(key, 14), (BATCH, 4), 0, CLASSES, dtype=jnp.int32)
    active_count = jax.random.randint(jax.random.fold_in(key, 15), (BATCH, 1), 2, 5, dtype=jnp.int32)
    active = (jnp.arange(4, dtype=jnp.int32)[None, :] < active_count).astype(jnp.float32)
    own_lo, own_hi, neg_lo, neg_hi = (0.6, 0.9, 0.3, 0.5)
    weights = jax.random.uniform(jax.random.fold_in(key, 16), (BATCH, 4), jnp.float32, neg_lo, neg_hi) * active
    own = jax.random.uniform(jax.random.fold_in(key, 17), (BATCH, 1), jnp.float32, own_lo, own_hi)
    mixed = own * unit[labels]
    for slot in range(4):
        mixed = mixed + weights[:, slot:slot + 1] * unit[negatives[:, slot]]
    noise_key = jax.random.fold_in(key, 18)
    noise = jax.random.normal(noise_key, (BATCH, D), jnp.float32)
    values = math.sqrt(D) * (mixed + 0.3 * noise / math.sqrt(D))
    return jnp.clip(values, -16.0, 16.0).astype(jnp.bfloat16)


def setup_inputs(seed: int = 0) -> dict:
    keys = jax.random.split(jax.random.key(seed), 4)
    return {
        "embeddings": draw_embeddings(jax.random.fold_in(keys[3], 71), 0),
        "centers": draw_centers(jax.random.fold_in(keys[3], 71), 0),
        "labels": draw_labels(jax.random.fold_in(keys[3], 71), 0),
    }


EPSILON = 1e-06
LOGIT_SCALE = 30.0
MARGIN = 0.5

def unit_rows(matrix):
    values = matrix.astype(jnp.float32)
    return (values * lax.rsqrt(lax.optimization_barrier(jnp.sum(values * values, axis=1, keepdims=True)) + EPSILON)).astype(jnp.bfloat16)

def margin_loss(other_sum, target_cos):
    sine = jnp.sqrt(jnp.maximum(1.0 - target_cos * target_cos, 0.0))
    shifted = target_cos * math.cos(MARGIN) - sine * math.sin(MARGIN)
    return LOGIT_SCALE + jnp.log(other_sum + jnp.exp(LOGIT_SCALE * shifted - LOGIT_SCALE)) - LOGIT_SCALE * shifted

def block_terms(rows, row_labels, centers_block):
    cosine = jnp.dot(rows, centers_block.T, preferred_element_type=jnp.float32)
    columns = jnp.arange(centers_block.shape[0], dtype=jnp.int32)
    is_target = row_labels[:, None] == columns[None, :]
    other_sum = lax.optimization_barrier(jnp.sum(jnp.where(is_target, 0.0, jnp.exp(LOGIT_SCALE * cosine - LOGIT_SCALE)), axis=1))
    target_cos = lax.optimization_barrier(jnp.sum(jnp.where(is_target, cosine, 0.0), axis=1))
    return (other_sum, target_cos)

def reference(embeddings, centers, labels):
    emb_unit = unit_rows(embeddings)
    center_unit = unit_rows(centers)
    span_rows = math.gcd(BATCH, 1024)
    emb_blocks = emb_unit.reshape(-1, span_rows, D)
    label_blocks = labels.reshape(-1, span_rows)

    def one_block(pair):
        return block_terms(pair[0], pair[1], center_unit)
    other_sum, target_cos = lax.map(one_block, (emb_blocks, label_blocks))
    return margin_loss(other_sum.reshape(-1), target_cos.reshape(-1))
```

```python
import functools
import math

import jax
import jax.numpy as jnp
from jax import lax
from jax.experimental import pallas as pl
from jax.experimental.pallas import tpu as pltpu
from jax.sharding import Mesh
from jax.sharding import PartitionSpec as P

AXES = ("x", "z", "yl", "yh", "c")
GROUP = ("x", "yl", "yh")
X, Y, Z, CORE = ("x",), ("yl", "yh"), ("z",), ("c",)
EPSILON = 1e-06
LOGIT_SCALE = 30.0
MARGIN = 0.5
SCALE2 = LOGIT_SCALE / math.log(2.0)
TILE = 512
NT = (((1,), (1,)), ((), ()))
MIB = 1024 * 1024


def unit_block(ref):
    values = ref[...].astype(jnp.float32)
    total = jnp.sum(values * values, axis=1, keepdims=True)
    return (values * lax.rsqrt(total + EPSILON)).astype(jnp.bfloat16)


def unit_kernel(e_ref, c_ref, a_ref, b_ref, u_ref):
    half = a_ref.shape[0]
    u_ref[...] = unit_block(c_ref)
    e = unit_block(e_ref)
    a_ref[...] = e[:half]
    b_ref[...] = e[half:]


def normalized(embeddings, centers):
    half = (embeddings.shape[0] // 2, embeddings.shape[1])
    shapes = [half, half, centers.shape]
    return pl.pallas_call(
        unit_kernel,
        out_shape=[jax.ShapeDtypeStruct(s, jnp.bfloat16) for s in shapes],
    )(embeddings, centers)


def add_terms(x_ref, first, rel, s, t):
    for j in range(TILE // 8):
        x = x_ref[first + 8 * j : first + 8 * j + 8, :]
        at_label = rel == 8 * j
        s = s + jnp.where(at_label, 0.0, jnp.exp2(x * SCALE2))
        t = jnp.where(at_label, x, t)
    return s, t


def terms_kernel(
    n_a, n_e, n_c, plan, owner_ref, base_ref, lab_ref, acc_ref, *refs
):
    e_refs, c_refs = refs[:n_e], refs[n_e : n_e + n_c]
    out_ref, e_buf, c_buf, even, odd, sems = refs[n_e + n_c :]
    copies = [
        pltpu.make_async_copy(ref, e_buf.at[pl.ds(i * TILE, TILE)], sems.at[i])
        for i, ref in enumerate(e_refs)
    ] + [
        pltpu.make_async_copy(ref, c_buf.at[pl.ds(i * TILE, TILE)], sems.at[n_e + i])
        for i, ref in enumerate(c_refs)
    ]
    for copy in copies:
        copy.start()
    if acc_ref is None:
        out_ref[...] = jnp.zeros_like(out_ref)
    else:
        out_ref[...] = acc_ref[...]
    for copy in copies:
        copy.wait()
    sub = lax.broadcasted_iota(jnp.int32, (8, TILE), 0)

    def product(r, k):
        rows = e_buf[pl.ds(pl.multiple_of(r * TILE, TILE), TILE), :]
        block = c_buf[pl.ds(pl.multiple_of(k * 2 * TILE, 2 * TILE), 2 * TILE), :]
        return lax.dot_general(block, rows, NT, preferred_element_type=jnp.float32)

    for e_lo, e_hi, k_lo, k_hi in plan:

        def one_tile(r, _, e_hi=e_hi, k_lo=k_lo, k_hi=k_hi):
            lanes = pl.ds(pl.multiple_of((r >= n_a).astype(jnp.int32) * 128, 128), 128)
            owners = [owner_ref[r * 4 + i] for i in range(4)]
            lab = jnp.concatenate([lab_ref[owners[i], :, lanes] for i in range(4)], axis=1)
            lab = lab - sub

            def add(x_ref, k, s, t):
                s, t = add_terms(x_ref, 0, lab - base_ref[2 * k], s, t)
                return add_terms(x_ref, TILE, lab - base_ref[2 * k + 1], s, t)

            def step(i, carry):
                s, t = carry
                k = k_lo + 2 * i
                odd[...] = product(r, k + 1)
                s, t = add(even, k, s, t)
                last = k + 2 >= k_hi
                even[...] = product(
                    jnp.where(last, jnp.minimum(r + 1, e_hi - 1), r),
                    jnp.where(last, k_lo, k + 2),
                )
                return add(odd, k + 1, s, t)

            zeros = jnp.zeros((8, TILE), jnp.float32)
            n = k_hi - k_lo
            if n == 1:
                s, t = add(even, k_lo, zeros, zeros)
                even[...] = product(jnp.minimum(r + 1, e_hi - 1), k_lo)
            else:
                s, t = lax.fori_loop(0, n // 2, step, (zeros, zeros))
            s = jnp.sum(s, axis=0, keepdims=True)
            t = jnp.sum(t, axis=0, keepdims=True)
            for i in range(4):
                part = slice(128 * i, 128 * i + 128)
                out_ref[owners[i], 0:1, lanes] += s[:, part]
                out_ref[owners[i], 1:2, lanes] += t[:, part]
            return 0

        even[...] = product(e_lo, k_lo)
        lax.fori_loop(e_lo, e_hi, one_tile, 0)


def terms(acc, pieces_a, pieces_b, classes, plan, labels):
    rows = [p for p, _ in pieces_a + pieces_b]
    owners = jnp.stack([o for _, own in pieces_a + pieces_b for o in own])
    bases = jnp.stack([b for _, b in classes])
    n_e, n_c = len(rows), len(classes)
    kernel = functools.partial(terms_kernel, len(pieces_a), n_e, n_c, plan)
    first = acc is None
    if first:
        kernel = functools.partial(lambda k, o, b, l, *refs: k(o, b, l, None, *refs), kernel)
    smem = pl.BlockSpec(memory_space=pltpu.SMEM)
    vmem = pl.BlockSpec(memory_space=pltpu.VMEM)
    blocks = sum((e1 - e0) * (k1 - k0) * 2 for e0, e1, k0, k1 in plan)
    return pl.pallas_call(
        kernel,
        out_shape=jax.ShapeDtypeStruct((16, 2, 256), jnp.float32),
        in_specs=[smem, smem, vmem]
        + [vmem] * (not first)
        + [pl.BlockSpec(memory_space=pl.ANY)] * (n_e + n_c),
        out_specs=vmem,
        scratch_shapes=[
            pltpu.VMEM((n_e * TILE, 512), jnp.bfloat16),
            pltpu.VMEM((n_c * TILE, 512), jnp.bfloat16),
            pltpu.VMEM((2 * TILE, TILE), jnp.float32),
            pltpu.VMEM((2 * TILE, TILE), jnp.float32),
            pltpu.SemaphoreType.DMA((n_e + n_c,)),
        ],
        compiler_params=pltpu.CompilerParams(vmem_limit_bytes=32 * MIB),
        cost_estimate=pl.CostEstimate(
            flops=blocks * 2 * TILE**3,
            bytes_accessed=(n_e + n_c) * TILE * 1024,
            transcendentals=blocks * TILE * TILE,
        ),
    )(owners, bases, labels, *([] if first else [acc]), *rows, *[p for p, _ in classes])


def shift(x, axes, by):
    def place(i):
        return (i % 2) * 2 + i // 2 if axes == Y else i

    n = lax.axis_size(axes)
    return lax.ppermute(x, axes, [(place(i), place((i + by) % n)) for i in range(n)])


def ring(x, axes):
    up, down = shift(x, axes, 1), shift(x, axes, -1)
    return up, down, shift(up, axes, 1)


def body(embeddings, centers, labels):
    a, b, c = normalized(embeddings, centers)
    x, z, c_i = lax.axis_index("x"), lax.axis_index("z"), lax.axis_index("c")
    yl, yh = lax.axis_index("yl"), lax.axis_index("yh")
    y = yh * 2 + yl

    def owner(dx, dy):
        ys = (y - dy) % 4
        return (x - dx) % 4 * 4 + ys % 2 * 2 + ys // 2

    def base(dz, other):
        core = 1 - c_i if other else c_i
        return ((((x * 4 + (z - dz) % 4) * 2 + yl) * 2 + yh) * 2 + core) * 512

    order = (0, 1, -1, 2)
    a_ring = ring(a, Y)
    b_ring = ring(b, X)
    c_ring = ring(c, Z)
    lab = lax.all_to_all(
        jnp.broadcast_to(labels[None, None], (16, 1, 256)), GROUP, 0, 0, tiled=True
    )
    a_all = jnp.concatenate([a, *a_ring])
    b_all = jnp.concatenate([b, *b_ring])
    classes = []
    for dz, piece in zip(order, (c, *c_ring)):
        classes.append((piece, base(dz, False)))
        classes.append((shift(piece, CORE, 1), base(dz, True)))
    a_rings = [(p, [owner(dx, dy) for dy in order]) for dx, p in zip(order, (a_all, *ring(a_all, X)))]
    b_rings = [(p, [owner(dx, dy) for dx in order]) for dy, p in zip(order, (b_all, *ring(b_all, Y)))]
    acc = terms(None, a_rings[:1], b_rings[:1], classes, ((0, 2, 0, 4),), lab)
    acc = terms(acc, a_rings[1:3], b_rings[1:3], classes, ((0, 4, 0, 4),), lab)
    acc = terms(acc, a_rings[3:], b_rings[3:], classes, ((0, 2, 0, 4),), lab)
    parts = lax.all_to_all(acc, GROUP, 0, 0, tiled=True)
    sums = jnp.sum(parts, axis=0)
    return margin_loss(sums[0], sums[1])


def margin_loss(other_sum, target_cos):
    sine = jnp.sqrt(jnp.maximum(1.0 - target_cos * target_cos, 0.0))
    shifted = target_cos * math.cos(MARGIN) - sine * math.sin(MARGIN)
    return jnp.log(other_sum + jnp.exp(LOGIT_SCALE * shifted)) - LOGIT_SCALE * shifted


def solution(mesh):
    finer = Mesh(mesh.devices.reshape(4, 4, 2, 2, 2), AXES)
    rows = ("yh", "c", "x", "z", "yl")
    placed = (P(rows, None), P(AXES, None), P(rows))
    return jax.shard_map(body, mesh=finer, in_specs=placed, out_specs=P(rows), check_vma=False)
```

```python
import functools
import math

import jax
import jax.numpy as jnp
from jax import lax
from jax.experimental import pallas as pl
from jax.experimental.pallas import tpu as pltpu
from jax.sharding import Mesh
from jax.sharding import PartitionSpec as P

AXES = ("x", "z", "yl", "yh", "c")
CHIPS = ("x", "yl", "yh")
DEVICES = ("x", "yl", "yh", "c")
EPSILON = 1e-06
LOGIT_SCALE = 30.0
MARGIN = 0.5
SCALE2 = LOGIT_SCALE / math.log(2.0)
TILE = 512
ROWS = 256
PITCH = 272
NT = (((1,), (1,)), ((), ()))
MIB = 1024 * 1024
OFFSETS = (0, 1, -1, 2)


def unit_block(ref):
    values = ref[...].astype(jnp.float32)
    total = jnp.sum(values * values, axis=1, keepdims=True)
    return (values * lax.rsqrt(total + EPSILON)).astype(jnp.bfloat16)


def unit_kernel(e_ref, c_ref, l_ref, a_ref, u_ref):
    u_ref[...] = unit_block(c_ref)
    a_ref[:ROWS, :] = unit_block(e_ref)
    label = jnp.concatenate([l_ref[...] // 256, l_ref[...] % 256], axis=1)
    label = jnp.broadcast_to(label.astype(jnp.float32), (PITCH - ROWS, 2 * ROWS))
    a_ref[ROWS:, :] = label.astype(jnp.bfloat16)


def normalized(embeddings, centers, labels):
    shapes = [(PITCH, embeddings.shape[1]), centers.shape]
    return pl.pallas_call(
        unit_kernel,
        out_shape=[jax.ShapeDtypeStruct(s, jnp.bfloat16) for s in shapes],
    )(embeddings, centers, labels.reshape(1, ROWS))


def add_terms(x_ref, first, rel, s, t):
    ss, tt = [s, None], [t, None]
    for j in range(TILE // 8):
        x = x_ref[first + 8 * j : first + 8 * j + 8, :]
        at_label = rel == 8 * j
        e = jnp.where(at_label, 0.0, jnp.exp2(x * SCALE2))
        i = j % 2
        ss[i] = e if ss[i] is None else ss[i] + e
        tt[i] = jnp.where(at_label, x, 0.0 if tt[i] is None else tt[i])
    return ss[0] + ss[1], tt[0] + tt[1]


def terms_kernel(tiles, n_c, plan, first, last, owner_ref, base_ref, *refs):
    refs = list(refs)
    if not first:
        refs.pop(0)
    n_e = len(tiles)
    e_refs, c_refs = refs[: n_e // 2], refs[n_e // 2 : n_e // 2 + n_c]
    refs = refs[n_e // 2 + n_c :]
    acc_ref = refs.pop(0)
    outs = [refs.pop(0) for _ in range(2 * last)]
    e_buf, l_buf, c_buf, even, odd, sems = refs

    def rows_copies(tile, ref, base):
        copies = []
        for i in range(2):
            n = tile * 2 + i
            rows = e_buf.at[pl.ds(pl.multiple_of(n * ROWS, ROWS), ROWS)]
            copies.append((ref.at[pl.ds(base + i * PITCH, ROWS)], rows, sems.at[n]))
            labels = ref.at[pl.ds(base + i * PITCH + ROWS, PITCH - ROWS)]
            copies.append((labels, l_buf.at[n], sems.at[2 * n_e + n]))
        return [pltpu.make_async_copy(*c) for c in copies]

    classes = [
        pltpu.make_async_copy(ref, c_buf.at[pl.ds(i * TILE, TILE)], sems.at[4 * n_e + i])
        for i, ref in enumerate(c_refs)
    ]
    start = plan[0][2]
    order = classes[2 * start : 2 * start + 2], classes[: 2 * start] + classes[2 * start + 2 :]
    for copy in order[0] + rows_copies(0, e_refs[0], 0) + order[1]:
        copy.start()
    for i in range(1, n_e):
        for copy in rows_copies(i, e_refs[i // 2], i % 2 * 2 * PITCH):
            copy.start()
    if first:
        acc_ref[...] = jnp.zeros_like(acc_ref)
    sub = lax.broadcasted_iota(jnp.int32, (8, TILE), 0)

    def arrived(tile):
        for copy in rows_copies(tile, e_refs[0], 0):
            copy.wait()

    def product(r, k):
        rows = e_buf[pl.ds(pl.multiple_of(r * TILE, TILE), TILE), :]
        block = c_buf[pl.ds(pl.multiple_of(k * 2 * TILE, 2 * TILE), 2 * TILE), :]
        return lax.dot_general(block, rows, NT, preferred_element_type=jnp.float32)

    def add(x_ref, r, k):
        owners = [owner_ref[(tiles[0] + r) * 2 + i] for i in range(2)]
        halves = [l_buf[2 * r + i].astype(jnp.float32)[:1].astype(jnp.int32) for i in range(2)]
        lab = jnp.concatenate([h[:, :ROWS] * 256 + h[:, ROWS:] for h in halves], axis=1) - sub
        zeros = jnp.zeros((8, TILE), jnp.float32)
        s, t = add_terms(x_ref, 0, lab - base_ref[2 * k], zeros, zeros)
        s, t = add_terms(x_ref, TILE, lab - base_ref[2 * k + 1], s, t)
        for i, o in enumerate(owners):
            acc_ref[o, 0:8, :] += s[:, 256 * i : 256 * i + 256]
            acc_ref[o, 8:16, :] += t[:, 256 * i : 256 * i + 256]

    for segment, (e_lo, e_hi, k_lo, k_hi) in enumerate(plan):
        n_k = k_hi - k_lo

        def step(i, more, e_lo=e_lo, k_lo=k_lo, n_k=n_k):
            if n_k == 1:
                now, then, new = e_lo + 2 * i, e_lo + 2 * i + 1, e_lo + 2 * i + 2
                arrived(then)
                ks = (k_lo, k_lo)
            else:
                now = then = e_lo + i
                new = now + 1
                ks = (k_lo, k_lo + 1)
            if more:
                arrived(new)
            odd[...] = product(then, ks[1])
            add(even, now, ks[0])
            if more:
                even[...] = product(new, k_lo)
            add(odd, then, ks[1])

        arrived(e_lo)
        if segment == 0:
            for copy in order[0]:
                copy.wait()
        even[...] = product(e_lo, k_lo)
        if segment == 0:
            for copy in order[1]:
                copy.wait()
        n = (e_hi - e_lo) * n_k // 2
        lax.fori_loop(0, n - 1, lambda i, _, step=step: step(i, True) or 0, 0)
        step(n - 1, False)

    for which, out in enumerate(outs):
        for g in range(16):
            for i in range(2):
                part = acc_ref[2 * g + which, 8 * i : 8 * i + 8, :]
                out[g, i : i + 1, :] = jnp.sum(part, axis=0, keepdims=True)


def terms(acc, tiles, rows, classes, plan, owners, bases, last=False):
    n_e, n_c, first = len(tiles), len(classes), acc is None
    smem = pl.BlockSpec(memory_space=pltpu.SMEM)
    vmem = pl.BlockSpec(memory_space=pltpu.VMEM)
    blocks = sum((e1 - e0) * (k1 - k0) * 2 for e0, e1, k0, k1 in plan)
    sums = jax.ShapeDtypeStruct((16, 2, 256), jnp.float32)
    out = pl.pallas_call(
        functools.partial(terms_kernel, tiles, n_c, plan, first, last),
        out_shape=[jax.ShapeDtypeStruct((32, 16, 256), jnp.float32)] + [sums] * (2 * last),
        in_specs=[smem, smem]
        + [vmem] * (not first)
        + [pl.BlockSpec(memory_space=pl.ANY)] * (len(rows) + n_c),
        out_specs=[vmem] * (1 + 2 * last),
        scratch_shapes=[
            pltpu.VMEM((n_e * TILE, 512), jnp.bfloat16),
            pltpu.VMEM((n_e * 2, PITCH - ROWS, 512), jnp.bfloat16),
            pltpu.VMEM((n_c * TILE, 512), jnp.bfloat16),
            pltpu.VMEM((2 * TILE, TILE), jnp.float32),
            pltpu.VMEM((2 * TILE, TILE), jnp.float32),
            pltpu.SemaphoreType.DMA((4 * n_e + n_c,)),
        ],
        input_output_aliases={} if first else {2: 0},
        compiler_params=pltpu.CompilerParams(vmem_limit_bytes=24 * MIB),
        cost_estimate=pl.CostEstimate(
            flops=blocks * 2 * TILE**3,
            bytes_accessed=(n_e + n_c) * TILE * 1024,
            transcendentals=blocks * TILE * TILE,
        ),
    )(owners, bases, *([] if first else [acc]), *rows, *classes)
    return out[1:] if last else out[0]


def cross(x, way, by):
    pairs = []
    for i in range(4):
        for y in range(4):
            for core in range(2):
                j, v = (i, (y + by) % 4) if core == way else ((i + by) % 4, y)
                pairs.append((place(i, y) * 2 + core, place(j, v) * 2 + core))
    return lax.ppermute(x, DEVICES, pairs)


def place(x, y):
    return x * 4 + y % 2 * 2 + y // 2


def swap(x):
    return lax.ppermute(x, "c", [(0, 1), (1, 0)])


def up_z(x, by):
    return lax.ppermute(x, "z", [(i, (i + by) % 4) for i in range(4)])


def body(embeddings, centers, labels):
    x, z, core = lax.axis_index("x"), lax.axis_index("z"), lax.axis_index("c")
    yl, yh = lax.axis_index("yl"), lax.axis_index("yh")
    y = yh * 2 + yl

    e, c = normalized(embeddings, centers, labels)
    c_up = up_z(c, 1)
    e_up, e_down, e_far = cross(e, 0, 1), cross(e, 0, -1), cross(e, 0, 2)
    e_up, e_down, e_far, c_up = lax.optimization_barrier((e_up, e_down, e_far, c_up))
    own = jnp.concatenate([e, e_up, e_down, e_far])
    up, down = cross(own, 1, 1), cross(own, 1, -1)
    c_far, c_down = up_z(c_up, 1), up_z(c, -1)
    classes = (c, c_up, c_down, c_far)

    kinds = ((0, 0), (0, 1), (1, 0), (-1, 0), (1, 1), (-1, 1), (2, 1), (2, 0))
    second = jnp.array([d for d, _ in kinds for _ in OFFSETS], jnp.int32)
    first = jnp.array([o for _ in kinds for o in OFFSETS], jnp.int32)
    other = jnp.array([w for _, w in kinds for _ in OFFSETS], jnp.int32)
    along_y = (core + other) % 2 == 0
    gx = (x - jnp.where(along_y, second, first) + 4) % 4
    gy = (y - jnp.where(along_y, first, second) + 4) % 4
    owners = (gx * 4 + gy % 2 * 2 + gy // 2) * 2 + other
    at_z = (z - jnp.array((0, 1, -1, 2), jnp.int32) + 4) % 4
    bases = ((((x * 4 + at_z) * 2 + yl) * 2 + yh) * 2 + core) * TILE

    def run(acc, tiles, rows, n_c, plan, last=False):
        return terms(acc, tiles, rows, classes[:n_c], plan, owners, bases, last)

    own_swapped = swap(own)
    acc = run(None, range(0, 4), (own, own_swapped), 2, ((0, 4, 0, 1),))
    acc, up = lax.optimization_barrier((acc, up))
    far = cross(up, 1, 1)
    rows = (own, own_swapped, up, down)
    acc = run(acc, range(0, 8), rows, 4, ((0, 4, 1, 2), (4, 8, 0, 2)))
    acc, far = lax.optimization_barrier((acc, far))
    up_swapped, down_swapped = swap(up), swap(down)
    acc = run(acc, range(8, 12), (up_swapped, down_swapped), 4, ((0, 4, 0, 2),))
    mine, others = run(acc, range(12, 16), (swap(far), far), 4, ((0, 4, 0, 2),), True)
    mine = mine + swap(others)
    parts = lax.all_to_all(mine, CHIPS, 0, 0, tiled=True)
    sums = jnp.sum(parts, axis=0)
    return margin_loss(sums[0], sums[1])


def margin_loss(other_sum, target_cos):
    sine = jnp.sqrt(jnp.maximum(1.0 - target_cos * target_cos, 0.0))
    shifted = target_cos * math.cos(MARGIN) - sine * math.sin(MARGIN)
    return jnp.log(other_sum + jnp.exp(LOGIT_SCALE * shifted)) - LOGIT_SCALE * shifted


def solution(mesh):
    finer = Mesh(mesh.devices.reshape(4, 4, 2, 2, 2), AXES)
    rows = ("yh", "c", "x", "z", "yl")
    placed = (P(rows, None), P(AXES, None), P(rows))
    return jax.shard_map(body, mesh=finer, in_specs=placed, out_specs=P(rows), check_vma=False)
```

```python
import functools
import math

import jax
import jax.numpy as jnp
from jax import lax
from jax.experimental import pallas as pl
from jax.experimental.pallas import tpu as pltpu
from jax.sharding import Mesh
from jax.sharding import PartitionSpec as P

AXES = ("x", "z", "yl", "yh", "c")
CHIPS = ("x", "yl", "yh")
DEVICES = ("x", "yl", "yh", "c")
EPSILON = 1e-06
LOGIT_SCALE = 30.0
MARGIN = 0.5
SCALE2 = LOGIT_SCALE / math.log(2.0)
TILE = 512
WIDE = 1024
PARTS = 4
ROWS = 256
PITCH = 272
NT = (((1,), (1,)), ((), ()))
MIB = 1024 * 1024
OFFSETS = (0, 1, -1, 2)


def unit_block(ref):
    values = ref[...].astype(jnp.float32)
    total = jnp.sum(values * values, axis=1, keepdims=True)
    return (values * lax.rsqrt(total + EPSILON)).astype(jnp.bfloat16)


def unit_kernel(e_ref, c_ref, l_ref, a_ref, u_ref):
    u_ref[...] = unit_block(c_ref)
    a_ref[:ROWS, :] = unit_block(e_ref)
    label = jnp.concatenate([l_ref[...] // 256, l_ref[...] % 256], axis=1)
    label = jnp.broadcast_to(label.astype(jnp.float32), (PITCH - ROWS, 2 * ROWS))
    a_ref[ROWS:, :] = label.astype(jnp.bfloat16)


def normalized(embeddings, centers, labels):
    shapes = [(PITCH, embeddings.shape[1]), centers.shape]
    return pl.pallas_call(
        unit_kernel,
        out_shape=[jax.ShapeDtypeStruct(s, jnp.bfloat16) for s in shapes],
    )(embeddings, centers, labels.reshape(1, ROWS))


def add_terms(x_ref, rel):
    ss, tt = [0.0, 0.0], [0.0, 0.0]
    for j in range(TILE // 8):
        x = x_ref[8 * j : 8 * j + 8, :]
        at_label = rel == 8 * j
        e = jnp.where(at_label, 0.0, jnp.exp2(x * SCALE2))
        i = j % 2
        ss[i] = ss[i] + e
        tt[i] = jnp.where(at_label, x, tt[i])
    return ss[0] + ss[1], tt[0] + tt[1]


def steps_of(plan):
    rows, seen_r, seen_k = [], set(), set()
    for tiles, pieces in plan:
        for r in tiles:
            for k in pieces:
                rows.append((r, k, int(r not in seen_r), int(k not in seen_k)))
                seen_r.add(r)
                seen_k.add(k)
    return rows


def terms_kernel(shares, n_c, n_steps, at_owner, at_step, first, last, info_ref, *refs):
    refs = list(refs)
    if not first:
        refs.pop(0)
    n_e = len(shares)
    e_refs = [[refs.pop(0) for _ in range(n)] for n in shares]
    c_refs = [refs.pop(0) for _ in range(n_c)]
    acc_ref = refs.pop(0)
    outs = [refs.pop(0) for _ in range(2 * last)]
    e_buf, l_buf, c_buf, even, odd, sems = refs

    def part_copies(n, ref, first_row):
        rows = e_buf.at[pl.ds(pl.multiple_of(n * ROWS, ROWS), ROWS)]
        labels = ref.at[pl.ds(first_row + ROWS, PITCH - ROWS)]
        return [
            pltpu.make_async_copy(ref.at[pl.ds(first_row, ROWS)], rows, sems.at[n]),
            pltpu.make_async_copy(labels, l_buf.at[n], sems.at[PARTS * n_e + n]),
        ]

    def rows_copies(tile):
        copies = []
        for i in range(PARTS):
            each = PARTS // shares[tile]
            ref = e_refs[tile][i // each]
            copies += part_copies(tile * PARTS + i, ref, i % each * PITCH)
        return copies

    def class_copy(k, ref):
        here = c_buf.at[pl.ds(pl.multiple_of(k * TILE, TILE), TILE)]
        return pltpu.make_async_copy(ref, here, sems.at[2 * PARTS * n_e + k])

    def entry(step, which):
        return info_ref[at_step + 4 * step + which]

    starts = [[class_copy(k, ref)] for k, ref in enumerate(c_refs)]
    starts[1:1] = [rows_copies(0)]
    starts += [rows_copies(r) for r in range(1, n_e)]
    for copies in starts:
        for copy in copies:
            copy.start()
    if first:
        acc_ref[...] = jnp.zeros_like(acc_ref)
    sub = lax.broadcasted_iota(jnp.int32, (8, WIDE), 0)

    def arrived(step):
        @pl.when(entry(step, 2) == 1)
        def _():
            for i in range(PARTS):
                for copy in part_copies(entry(step, 0) * PARTS + i, e_refs[0][0], 0):
                    copy.wait()

        @pl.when(entry(step, 3) == 1)
        def _():
            class_copy(entry(step, 1), c_refs[0]).wait()

    def product(step):
        rows = e_buf[pl.ds(pl.multiple_of(entry(step, 0) * WIDE, WIDE), WIDE), :]
        block = c_buf[pl.ds(pl.multiple_of(entry(step, 1) * TILE, TILE), TILE), :]
        return lax.dot_general(block, rows, NT, preferred_element_type=jnp.float32)

    def add(x_ref, step):
        n = entry(step, 0) * PARTS
        parts = [l_buf[n + i].astype(jnp.float32)[:1].astype(jnp.int32) for i in range(PARTS)]
        lab = jnp.concatenate([h[:, :ROWS] * 256 + h[:, ROWS:] for h in parts], axis=1)
        s, t = add_terms(x_ref, lab - sub - info_ref[entry(step, 1)])
        for i in range(PARTS):
            o = info_ref[at_owner + n + i]
            acc_ref[o, 0:8, :] += s[:, ROWS * i : ROWS * i + ROWS]
            acc_ref[o, 8:16, :] += t[:, ROWS * i : ROWS * i + ROWS]

    arrived(0)
    even[...] = product(0)

    def two_steps(i, _):
        step = 2 * i
        more = step + 2 < n_steps
        arrived(step + 1)
        pl.when(more)(lambda: arrived(step + 2))
        odd[...] = product(step + 1)
        add(even, step)

        even[...] = product(jnp.minimum(step + 2, n_steps - 1))
        add(odd, step + 1)
        return 0

    lax.fori_loop(0, n_steps // 2, two_steps, 0)

    for which, out in enumerate(outs):
        for g in range(16):
            for i in range(2):
                part = acc_ref[2 * g + which, 8 * i : 8 * i + 8, :]
                out[g, i : i + 1, :] = jnp.sum(part, axis=0, keepdims=True)


def terms(acc, tiles, classes, plan, info, at_owner, at_step, last=False):
    n_e, n_c, first = len(tiles), len(classes), acc is None
    rows = [piece for tile in tiles for piece in tile]
    smem = pl.BlockSpec(memory_space=pltpu.SMEM)
    vmem = pl.BlockSpec(memory_space=pltpu.VMEM)
    n_steps = len(steps_of(plan))
    sums = jax.ShapeDtypeStruct((16, 2, 256), jnp.float32)
    out = pl.pallas_call(
        functools.partial(terms_kernel, [len(t) for t in tiles], n_c, n_steps, at_owner, at_step, first, last),
        out_shape=[jax.ShapeDtypeStruct((32, 16, 256), jnp.float32)] + [sums] * (2 * last),
        in_specs=[smem] + [vmem] * (not first) + [pl.BlockSpec(memory_space=pl.ANY)] * (len(rows) + n_c),
        out_specs=[vmem] * (1 + 2 * last),
        scratch_shapes=[
            pltpu.VMEM((n_e * WIDE, 512), jnp.bfloat16),
            pltpu.VMEM((n_e * PARTS, PITCH - ROWS, 512), jnp.bfloat16),
            pltpu.VMEM((n_c * TILE, 512), jnp.bfloat16),
            pltpu.VMEM((TILE, WIDE), jnp.float32),
            pltpu.VMEM((TILE, WIDE), jnp.float32),
            pltpu.SemaphoreType.DMA((2 * PARTS * n_e + n_c,)),
        ],
        input_output_aliases={} if first else {1: 0},
        compiler_params=pltpu.CompilerParams(vmem_limit_bytes=(52 if first else 24) * MIB),
        cost_estimate=pl.CostEstimate(
            flops=n_steps * 2 * TILE * WIDE * 512,
            bytes_accessed=(2 * n_e + n_c) * TILE * 1024,
            transcendentals=n_steps * TILE * WIDE,
        ),
    )(info, *([] if first else [acc]), *rows, *classes)
    return out[1:] if last else out[0]


def cross(x, way, by):
    pairs = []
    for i in range(4):
        for y in range(4):
            for core in range(2):
                j, v = (i, (y + by) % 4) if core == way else ((i + by) % 4, y)
                pairs.append((place(i, y) * 2 + core, place(j, v) * 2 + core))
    return lax.ppermute(x, DEVICES, pairs)


def place(x, y):
    return x * 4 + y % 2 * 2 + y // 2


def swap(x):
    return lax.ppermute(x, "c", [(0, 1), (1, 0)])


def up_z(x, by):
    return lax.ppermute(x, "z", [(i, (i + by) % 4) for i in range(4)])


def body(embeddings, centers, labels):
    x, z, core = lax.axis_index("x"), lax.axis_index("z"), lax.axis_index("c")
    yl, yh = lax.axis_index("yl"), lax.axis_index("yh")
    y = yh * 2 + yl

    e, c = normalized(embeddings, centers, labels)
    c_up, c_down = up_z(c, 1), up_z(c, -1)
    e_up, e_down, e_far = cross(e, 0, 1), cross(e, 0, -1), cross(e, 0, 2)
    e_far, c_up, c_down, e_up, e_down = lax.optimization_barrier(
        (e_far, c_up, c_down, e_up, e_down)
    )
    own = jnp.concatenate([e, e_up, e_down, e_far])
    up, down = cross(own, 1, 1), cross(own, 1, -1)
    c_far = up_z(c_up, 1)
    classes = (c, c_up, c_down, c_far)

    kinds = ((0, 0), (0, 1), (1, 0), (-1, 0), (1, 1), (-1, 1), (2, 1), (2, 0))
    plans = (
        (((0, 1), (0, 1, 2)),),
        (((2, 3), (0, 1, 2, 3)), ((0, 1), (3,))),
        (((0, 1), (0, 1, 2, 3)),),
        (((0, 1), (0, 1, 2, 3)),),
    )
    firsts = (0, 0, 4, 6)
    second = jnp.array([d for d, _ in kinds for _ in OFFSETS], jnp.int32)
    first = jnp.array([o for _ in kinds for o in OFFSETS], jnp.int32)
    other = jnp.array([w for _, w in kinds for _ in OFFSETS], jnp.int32)
    along_y = (core + other) % 2 == 0
    gx = (x - jnp.where(along_y, second, first) + 4) % 4
    gy = (y - jnp.where(along_y, first, second) + 4) % 4
    owners = (gx * 4 + gy % 2 * 2 + gy // 2) * 2 + other
    at_z = (z - jnp.array((0, 1, -1, 2), jnp.int32) + 4) % 4
    bases = ((((x * 4 + at_z) * 2 + yl) * 2 + yh) * 2 + core) * TILE
    steps = [steps_of(plan) for plan in plans]
    table = jnp.array([n for rows in steps for row in rows for n in row], jnp.int32)
    info = jnp.concatenate([bases, owners, table])

    def run(acc, call, rows, n_c=4, last=False):
        at_step = 4 + len(kinds) * PARTS + sum(4 * len(r) for r in steps[:call])
        at_owner = 4 + firsts[call] * PARTS
        return terms(acc, rows, classes[:n_c], plans[call], info, at_owner, at_step, last)

    own_swapped = swap(own)
    acc = run(None, 0, ((own,), (own_swapped,)), 3)
    acc, up = lax.optimization_barrier((acc, up))
    half = up.shape[0] // 2
    far_a = cross(up[:half], 1, 1)
    down, c_far = lax.optimization_barrier((down, c_far))
    classes = (c, c_up, c_down, c_far)
    far_b = cross(down[half:], 1, -1)
    acc = run(acc, 1, ((own,), (own_swapped,), (up,), (down,)))
    acc, far_a, far_b = lax.optimization_barrier((acc, far_a, far_b))
    acc = run(acc, 2, ((swap(up),), (swap(down),)))
    far, far_swapped = (far_a, far_b), (swap(far_a), swap(far_b))
    mine, others = run(acc, 3, (far_swapped, far), last=True)
    mine = mine + swap(others)
    parts = lax.all_to_all(mine, CHIPS, 0, 0, tiled=True)
    sums = jnp.sum(parts, axis=0)
    return margin_loss(sums[0], sums[1])


def margin_loss(other_sum, target_cos):
    sine = jnp.sqrt(jnp.maximum(1.0 - target_cos * target_cos, 0.0))
    shifted = target_cos * math.cos(MARGIN) - sine * math.sin(MARGIN)
    return jnp.log(other_sum + jnp.exp(LOGIT_SCALE * shifted)) - LOGIT_SCALE * shifted


def solution(mesh):
    finer = Mesh(mesh.devices.reshape(4, 4, 2, 2, 2), AXES)
    rows = ("yh", "c", "x", "z", "yl")
    placed = (P(rows, None), P(AXES, None), P(rows))
    return jax.shard_map(body, mesh=finer, in_specs=placed, out_specs=P(rows), check_vma=False)
```

```python
import functools
import math

import jax
import jax.numpy as jnp
from jax import lax
from jax.experimental import pallas as pl
from jax.experimental.pallas import tpu as pltpu
from jax.sharding import Mesh
from jax.sharding import PartitionSpec as P

AXES = ("x", "z", "yl", "yh", "c")
DEVICES = ("x", "yl", "yh", "c")
EPSILON = 1e-06
LOGIT_SCALE = 30.0
MARGIN = 0.5
SCALE2 = LOGIT_SCALE / math.log(2.0)
TILE = 512
WIDE = 1024
PARTS = 4
ROWS = 256
PITCH = 272
NT = (((1,), (1,)), ((), ()))
MIB = 1024 * 1024
OFFSETS = (0, 1, -1, 2)


def unit_block(ref):
    values = ref[...].astype(jnp.float32)
    total = jnp.sum(values * values, axis=1, keepdims=True)
    return (values * lax.rsqrt(total + EPSILON)).astype(jnp.bfloat16)


def unit_kernel(e_ref, c_ref, l_ref, a_ref, u_ref):
    u_ref[...] = unit_block(c_ref)
    a_ref[:ROWS, :] = unit_block(e_ref)
    label = jnp.concatenate([l_ref[...] // 256, l_ref[...] % 256], axis=1)
    label = jnp.broadcast_to(label.astype(jnp.float32), (PITCH - ROWS, 2 * ROWS))
    a_ref[ROWS:, :] = label.astype(jnp.bfloat16)


def normalized(embeddings, centers, labels):
    shapes = [(PITCH, embeddings.shape[1]), centers.shape]
    return pl.pallas_call(
        unit_kernel,
        out_shape=[jax.ShapeDtypeStruct(s, jnp.bfloat16) for s in shapes],
    )(embeddings, centers, labels.reshape(1, ROWS))


def add_terms(x_ref, rel):
    ss, tt = [0.0, 0.0], [0.0, 0.0]
    for j in range(TILE // 8):
        x = x_ref[8 * j : 8 * j + 8, :]
        at_label = rel == 8 * j
        e = jnp.where(at_label, 0.0, jnp.exp2(x * SCALE2))
        i = j % 2
        ss[i] = ss[i] + e
        tt[i] = jnp.where(at_label, x, tt[i])
    return ss[0] + ss[1], tt[0] + tt[1]


def steps_of(plan):
    rows, seen_r, seen_k = [], set(), set()
    for tiles, pieces in plan:
        for r in tiles:
            for k in pieces:
                rows.append((r, k, int(r not in seen_r), int(k not in seen_k)))
                seen_r.add(r)
                seen_k.add(k)
    return rows


def terms_kernel(n_e, n_c, n_steps, at_owner, at_step, first, last, info_ref, *refs):
    refs = list(refs)
    if not first:
        refs.pop(0)
    e_refs = [refs.pop(0) for _ in range(n_e)]
    c_refs = [refs.pop(0) for _ in range(n_c)]
    acc_ref = refs.pop(0)
    out_ref = refs.pop(0) if last else None
    e_buf, l_buf, c_buf, even, odd, sems = refs

    def rows_copies(tile, ref):
        rows = e_buf.at[pl.ds(pl.multiple_of(tile * WIDE, WIDE), WIDE)]
        labels = ref.at[pl.ds(WIDE, PITCH - ROWS)]
        return [
            pltpu.make_async_copy(ref.at[pl.ds(0, WIDE)], rows, sems.at[tile]),
            pltpu.make_async_copy(labels, l_buf.at[tile], sems.at[n_e + tile]),
        ]

    def class_copy(k, ref):
        here = c_buf.at[pl.ds(pl.multiple_of(k * TILE, TILE), TILE)]
        return pltpu.make_async_copy(ref, here, sems.at[2 * n_e + k])

    def entry(step, which):
        return info_ref[at_step + 4 * step + which]

    starts = [[class_copy(k, ref)] for k, ref in enumerate(c_refs)]
    starts[1:1] = [rows_copies(0, e_refs[0])]
    starts += [rows_copies(r, e_refs[r]) for r in range(1, n_e)]
    for copies in starts:
        for copy in copies:
            copy.start()
    if first:
        acc_ref[...] = jnp.zeros_like(acc_ref)
    sub = lax.broadcasted_iota(jnp.int32, (8, WIDE), 0)

    def arrived(step):
        @pl.when(entry(step, 2) == 1)
        def _():
            for copy in rows_copies(entry(step, 0), e_refs[0]):
                copy.wait()

        @pl.when(entry(step, 3) == 1)
        def _():
            class_copy(entry(step, 1), c_refs[0]).wait()

    def product(step):
        rows = e_buf[pl.ds(pl.multiple_of(entry(step, 0) * WIDE, WIDE), WIDE), :]
        block = c_buf[pl.ds(pl.multiple_of(entry(step, 1) * TILE, TILE), TILE), :]
        return lax.dot_general(block, rows, NT, preferred_element_type=jnp.float32)

    def add(x_ref, step):
        n = entry(step, 0) * PARTS
        tile = l_buf[entry(step, 0)].astype(jnp.float32)
        parts = [tile[4 * i : 4 * i + 1].astype(jnp.int32) for i in range(PARTS)]
        lab = jnp.concatenate([h[:, :ROWS] * 256 + h[:, ROWS:] for h in parts], axis=1)
        s, t = add_terms(x_ref, lab - sub - info_ref[entry(step, 1)])
        for i in range(PARTS):
            o = info_ref[at_owner + n + i]
            acc_ref[o, 0:8, :] += s[:, ROWS * i : ROWS * i + ROWS]
            acc_ref[o, 8:16, :] += t[:, ROWS * i : ROWS * i + ROWS]

    arrived(0)
    even[...] = product(0)

    def two_steps(i, _):
        step = 2 * i
        more = step + 2 < n_steps
        arrived(step + 1)
        pl.when(more)(lambda: arrived(step + 2))
        odd[...] = product(step + 1)
        add(even, step)

        even[...] = product(jnp.minimum(step + 2, n_steps - 1))
        add(odd, step + 1)
        return 0

    lax.fori_loop(0, n_steps // 2, two_steps, 0)

    if last:
        core = info_ref[4]
        for o in range(32):
            for i in range(2):
                total = jnp.sum(acc_ref[o, 8 * i : 8 * i + 8, :], axis=0, keepdims=True)
                out_ref[o + core * (1 - 2 * (o % 2)), i : i + 1, :] = total


def terms(acc, tiles, classes, plan, info, at_owner, at_step, last=False):
    n_e, n_c, first = len(tiles), len(classes), acc is None
    rows = [piece for tile in tiles for piece in tile]
    smem = pl.BlockSpec(memory_space=pltpu.SMEM)
    vmem = pl.BlockSpec(memory_space=pltpu.VMEM)
    n_steps = len(steps_of(plan))
    sums = jax.ShapeDtypeStruct((32, 2, 256), jnp.float32)
    out = pl.pallas_call(
        functools.partial(terms_kernel, n_e, n_c, n_steps, at_owner, at_step, first, last),
        out_shape=[jax.ShapeDtypeStruct((32, 16, 256), jnp.float32)] + [sums] * last,
        in_specs=[smem] + [vmem] * (not first) + [pl.BlockSpec(memory_space=pl.ANY)] * (len(rows) + n_c),
        out_specs=[vmem] * (1 + last),
        scratch_shapes=[
            pltpu.VMEM((n_e * WIDE, 512), jnp.bfloat16),
            pltpu.VMEM((n_e, PITCH - ROWS, 512), jnp.bfloat16),
            pltpu.VMEM((n_c * TILE, 512), jnp.bfloat16),
            pltpu.VMEM((TILE, WIDE), jnp.float32),
            pltpu.VMEM((TILE, WIDE), jnp.float32),
            pltpu.SemaphoreType.DMA((2 * n_e + n_c,)),
        ],
        input_output_aliases={} if first else {1: 0},
        compiler_params=pltpu.CompilerParams(vmem_limit_bytes=24 * MIB),
        cost_estimate=pl.CostEstimate(
            flops=n_steps * 2 * TILE * WIDE * 512,
            bytes_accessed=(2 * n_e + n_c) * TILE * 1024,
            transcendentals=n_steps * TILE * WIDE,
        ),
    )(info, *([] if first else [acc]), *rows, *classes)
    return out[-1]


def cross(x, way, by):
    pairs = []
    for i in range(4):
        for y in range(4):
            for core in range(2):
                j, v = (i, (y + by) % 4) if core == way else ((i + by) % 4, y)
                pairs.append((place(i, y) * 2 + core, place(j, v) * 2 + core))
    return lax.ppermute(x, DEVICES, pairs)


def place(x, y):
    return x * 4 + y % 2 * 2 + y // 2


def swap(x):
    return lax.ppermute(x, "c", [(0, 1), (1, 0)])


def up_z(x, by):
    return lax.ppermute(x, "z", [(i, (i + by) % 4) for i in range(4)])


def body(embeddings, centers, labels):
    x, z, core = lax.axis_index("x"), lax.axis_index("z"), lax.axis_index("c")
    yl, yh = lax.axis_index("yl"), lax.axis_index("yh")
    y = yh * 2 + yl

    e, c = normalized(embeddings, centers, labels)
    c_up, c_down = up_z(c, 1), up_z(c, -1)
    e_up, e_down, e_far = cross(e, 0, 1), cross(e, 0, -1), cross(e, 0, 2)
    e_far, c_up, c_down, e_up, e_down = lax.optimization_barrier(
        (e_far, c_up, c_down, e_up, e_down)
    )
    parts = (e, e_up, e_down, e_far)
    below = [p[ROWS : ROWS + (PITCH - ROWS) // PARTS] for p in parts]
    own = jnp.concatenate([p[:ROWS] for p in parts] + below)
    up, down = cross(own, 1, 1), cross(own, 1, -1)
    c_far = up_z(c_up, 1)
    classes = (c, c_up, c_down, c_far)

    kinds = ((0, 0), (0, 1), (1, 0), (-1, 0), (1, 1), (-1, 1), (2, 0), (2, 1))
    plans = (
        (((0, 1), (0, 1, 2)),),
        (((2, 3), (0, 1, 2, 3)), ((0, 1), (3,))),
        (((0, 1), (0, 1, 2, 3)),),
        (((0,), (0, 1, 2, 3)),),
        (((0,), (0, 1, 2, 3)),),
    )
    firsts = (0, 0, 4, 6, 7)
    second = jnp.array([d for d, _ in kinds for _ in OFFSETS], jnp.int32)
    first = jnp.array([o for _ in kinds for o in OFFSETS], jnp.int32)
    other = jnp.array([w for _, w in kinds for _ in OFFSETS], jnp.int32)
    along_y = (core + other) % 2 == 0
    gx = (x - jnp.where(along_y, second, first) + 4) % 4
    gy = (y - jnp.where(along_y, first, second) + 4) % 4
    owners = (gx * 4 + gy % 2 * 2 + gy // 2) * 2 + other
    at_z = (z - jnp.array((0, 1, -1, 2), jnp.int32) + 4) % 4
    bases = ((((x * 4 + at_z) * 2 + yl) * 2 + yh) * 2 + core) * TILE
    steps = [steps_of(plan) for plan in plans]
    table = jnp.array([n for rows in steps for row in rows for n in row], jnp.int32)
    info = jnp.concatenate([bases, core[None], owners, table])

    def run(acc, call, rows, n_c=4, last=False):
        at_step = 5 + len(kinds) * PARTS + sum(4 * len(r) for r in steps[:call])
        at_owner = 5 + firsts[call] * PARTS
        return terms(acc, rows, classes[:n_c], plans[call], info, at_owner, at_step, last)

    own_swapped = swap(own)
    acc = run(None, 0, ((own,), (own_swapped,)), 3)
    acc, up = lax.optimization_barrier((acc, up))
    far = cross(up, 1, 1)
    down, c_far = lax.optimization_barrier((down, c_far))
    classes = (c, c_up, c_down, c_far)
    acc = run(acc, 1, ((own,), (own_swapped,), (up,), (down,)))
    acc = run(acc, 2, ((swap(up),), (swap(down),)))
    acc, far = lax.optimization_barrier((acc, far))
    acc = run(acc, 3, ((far,),))
    sums = run(acc, 4, ((swap(far),),), last=True)
    parts = lax.all_to_all(sums, DEVICES, 0, 0, tiled=True)
    sums = jnp.sum(parts, axis=0)
    return margin_loss(sums[0], sums[1])


def margin_loss(other_sum, target_cos):
    sine = jnp.sqrt(jnp.maximum(1.0 - target_cos * target_cos, 0.0))
    shifted = target_cos * math.cos(MARGIN) - sine * math.sin(MARGIN)
    return jnp.log(other_sum + jnp.exp(LOGIT_SCALE * shifted)) - LOGIT_SCALE * shifted


def solution(mesh):
    finer = Mesh(mesh.devices.reshape(4, 4, 2, 2, 2), AXES)
    rows = ("yh", "c", "x", "z", "yl")
    placed = (P(rows, None), P(AXES, None), P(rows))
    return jax.shard_map(body, mesh=finer, in_specs=placed, out_specs=P(rows), check_vma=False)
```

```python
import functools
import math

import jax
import jax.numpy as jnp
from jax import lax
from jax.experimental import pallas as pl
from jax.experimental.pallas import tpu as pltpu
from jax.sharding import Mesh
from jax.sharding import PartitionSpec as P

AXES = ("x", "z", "yl", "yh", "c")
DEVICES = ("x", "yl", "yh", "c")
EPSILON = 1e-06
LOGIT_SCALE = 30.0
MARGIN = 0.5
SCALE2 = LOGIT_SCALE / math.log(2.0)
TILE = 512
WIDE = 1024
PARTS = 4
ROWS = 256
PITCH = 272
NT = (((1,), (1,)), ((), ()))
MIB = 1024 * 1024
OFFSETS = (0, 1, -1, 2)


def unit_block(ref):
    values = ref[...].astype(jnp.float32)
    total = jnp.sum(values * values, axis=1, keepdims=True)
    return (values * lax.rsqrt(total + EPSILON)).astype(jnp.bfloat16)


def unit_kernel(e_ref, c_ref, l_ref, a_ref, u_ref):
    u_ref[...] = unit_block(c_ref)
    a_ref[:ROWS, :] = unit_block(e_ref)
    label = jnp.concatenate([l_ref[...] // 256, l_ref[...] % 256], axis=1)
    label = jnp.broadcast_to(label.astype(jnp.float32), (PITCH - ROWS, 2 * ROWS))
    a_ref[ROWS:, :] = label.astype(jnp.bfloat16)


def normalized(embeddings, centers, labels):
    shapes = [(PITCH, embeddings.shape[1]), centers.shape]
    return pl.pallas_call(
        unit_kernel,
        out_shape=[jax.ShapeDtypeStruct(s, jnp.bfloat16) for s in shapes],
    )(embeddings, centers, labels.reshape(1, ROWS))


def add_terms(x_ref, rel):
    ss, tt = [0.0, 0.0], [0.0, 0.0]
    for j in range(TILE // 8):
        x = x_ref[8 * j : 8 * j + 8, :]
        at_label = rel == 8 * j
        e = jnp.where(at_label, 0.0, jnp.exp2(x * SCALE2))
        i = j % 2
        ss[i] = ss[i] + e
        tt[i] = jnp.where(at_label, x, tt[i])
    return ss[0] + ss[1], tt[0] + tt[1]


def steps_of(plan):
    rows, seen_r, seen_k = [], set(), set()
    for tiles, pieces in plan:
        for r in tiles:
            for k in pieces:
                rows.append((r, k, int(r not in seen_r), int(k not in seen_k)))
                seen_r.add(r)
                seen_k.add(k)
    return rows


def terms_kernel(n_e, n_c, n_steps, at_owner, at_step, first, last, info_ref, *refs):
    refs = list(refs)
    if not first:
        refs.pop(0)
    e_refs = [refs.pop(0) for _ in range(n_e)]
    c_refs = [refs.pop(0) for _ in range(n_c)]
    acc_ref = refs.pop(0)
    out_ref = refs.pop(0) if last else None
    e_buf, l_buf, c_buf, even, odd, sems = refs

    def rows_copies(tile, ref):
        rows = e_buf.at[pl.ds(pl.multiple_of(tile * WIDE, WIDE), WIDE)]
        labels = ref.at[pl.ds(WIDE, PITCH - ROWS)]
        return [
            pltpu.make_async_copy(ref.at[pl.ds(0, WIDE)], rows, sems.at[tile]),
            pltpu.make_async_copy(labels, l_buf.at[tile], sems.at[n_e + tile]),
        ]

    def class_copy(k, ref):
        here = c_buf.at[pl.ds(pl.multiple_of(k * TILE, TILE), TILE)]
        return pltpu.make_async_copy(ref, here, sems.at[2 * n_e + k])

    def entry(step, which):
        return info_ref[at_step + 4 * step + which]

    starts = [[class_copy(k, ref)] for k, ref in enumerate(c_refs)]
    starts[1:1] = [rows_copies(0, e_refs[0])]
    starts += [rows_copies(r, e_refs[r]) for r in range(1, n_e)]
    for copies in starts:
        for copy in copies:
            copy.start()
    if first:
        acc_ref[...] = jnp.zeros_like(acc_ref)
    sub = lax.broadcasted_iota(jnp.int32, (8, WIDE), 0)

    def arrived(step):
        @pl.when(entry(step, 2) == 1)
        def _():
            for copy in rows_copies(entry(step, 0), e_refs[0]):
                copy.wait()

        @pl.when(entry(step, 3) == 1)
        def _():
            class_copy(entry(step, 1), c_refs[0]).wait()

    def product(step):
        rows = e_buf[pl.ds(pl.multiple_of(entry(step, 0) * WIDE, WIDE), WIDE), :]
        block = c_buf[pl.ds(pl.multiple_of(entry(step, 1) * TILE, TILE), TILE), :]
        return lax.dot_general(block, rows, NT, preferred_element_type=jnp.float32)

    def add(x_ref, step):
        n = entry(step, 0) * PARTS
        tile = l_buf[entry(step, 0)].astype(jnp.float32)
        parts = [tile[4 * i : 4 * i + 1].astype(jnp.int32) for i in range(PARTS)]
        lab = jnp.concatenate([h[:, :ROWS] * 256 + h[:, ROWS:] for h in parts], axis=1)
        s, t = add_terms(x_ref, lab - sub - info_ref[entry(step, 1)])
        for i in range(PARTS):
            o = info_ref[at_owner + n + i]
            acc_ref[o, 0:8, :] += s[:, ROWS * i : ROWS * i + ROWS]
            acc_ref[o, 8:16, :] += t[:, ROWS * i : ROWS * i + ROWS]

    arrived(0)
    even[...] = product(0)

    def two_steps(i, _):
        step = 2 * i
        more = step + 2 < n_steps
        arrived(step + 1)
        pl.when(more)(lambda: arrived(step + 2))
        odd[...] = product(step + 1)
        add(even, step)

        even[...] = product(jnp.minimum(step + 2, n_steps - 1))
        add(odd, step + 1)
        return 0

    lax.fori_loop(0, n_steps // 2, two_steps, 0)

    if last:
        core = info_ref[4]
        for o in range(32):
            for i in range(2):
                total = jnp.sum(acc_ref[o, 8 * i : 8 * i + 8, :], axis=0, keepdims=True)
                out_ref[o + core * (1 - 2 * (o % 2)), i : i + 1, :] = total


def terms(acc, tiles, classes, plan, info, at_owner, at_step, last=False):
    n_e, n_c, first = len(tiles), len(classes), acc is None
    rows = [piece for tile in tiles for piece in tile]
    smem = pl.BlockSpec(memory_space=pltpu.SMEM)
    vmem = pl.BlockSpec(memory_space=pltpu.VMEM)
    n_steps = len(steps_of(plan))
    sums = jax.ShapeDtypeStruct((32, 2, 256), jnp.float32)
    out = pl.pallas_call(
        functools.partial(terms_kernel, n_e, n_c, n_steps, at_owner, at_step, first, last),
        out_shape=[jax.ShapeDtypeStruct((32, 16, 256), jnp.float32)] + [sums] * last,
        in_specs=[smem] + [vmem] * (not first) + [pl.BlockSpec(memory_space=pl.ANY)] * (len(rows) + n_c),
        out_specs=[vmem] * (1 + last),
        scratch_shapes=[
            pltpu.VMEM((n_e * WIDE, 512), jnp.bfloat16),
            pltpu.VMEM((n_e, PITCH - ROWS, 512), jnp.bfloat16),
            pltpu.VMEM((n_c * TILE, 512), jnp.bfloat16),
            pltpu.VMEM((TILE, WIDE), jnp.float32),
            pltpu.VMEM((TILE, WIDE), jnp.float32),
            pltpu.SemaphoreType.DMA((2 * n_e + n_c,)),
        ],
        input_output_aliases={} if first else {1: 0},
        compiler_params=pltpu.CompilerParams(vmem_limit_bytes=24 * MIB),
        cost_estimate=pl.CostEstimate(
            flops=n_steps * 2 * TILE * WIDE * 512,
            bytes_accessed=(2 * n_e + n_c) * TILE * 1024,
            transcendentals=n_steps * TILE * WIDE,
        ),
    )(info, *([] if first else [acc]), *rows, *classes)
    return out[-1]


def cross(x, way, by):
    pairs = []
    for i in range(4):
        for y in range(4):
            for core in range(2):
                j, v = (i, (y + by) % 4) if core == way else ((i + by) % 4, y)
                pairs.append((place(i, y) * 2 + core, place(j, v) * 2 + core))
    return lax.ppermute(x, DEVICES, pairs)


def place(x, y):
    return x * 4 + y % 2 * 2 + y // 2


def swap(x):
    return lax.ppermute(x, "c", [(0, 1), (1, 0)])


def up_z(x, by):
    return lax.ppermute(x, "z", [(i, (i + by) % 4) for i in range(4)])


def body(embeddings, centers, labels):
    x, z, core = lax.axis_index("x"), lax.axis_index("z"), lax.axis_index("c")
    yl, yh = lax.axis_index("yl"), lax.axis_index("yh")
    y = yh * 2 + yl

    e, c = normalized(embeddings, centers, labels)
    c_up, c_down = up_z(c, 1), up_z(c, -1)
    e_up, e_down, e_far = cross(e, 0, 1), cross(e, 0, -1), cross(e, 0, 2)
    e_far, c_up, c_down, e_up, e_down = lax.optimization_barrier(
        (e_far, c_up, c_down, e_up, e_down)
    )
    parts = (e, e_up, e_down, e_far)
    below = [p[ROWS : ROWS + (PITCH - ROWS) // PARTS] for p in parts]
    own = jnp.concatenate([p[:ROWS] for p in parts] + below)
    up, down = cross(own, 1, 1), cross(own, 1, -1)
    c_far = up_z(c_up, 1)
    classes = (c, c_up, c_down, c_far)

    kinds = ((0, 0), (0, 1), (1, 0), (-1, 0), (1, 1), (-1, 1), (2, 0), (2, 1))
    plans = (
        (((0, 1), (0, 1, 2)),),
        (((2, 3), (0, 1, 2, 3)), ((0, 1), (3,))),
        (((0, 1), (0, 1, 2, 3)),),
        (((0,), (0, 1, 2, 3)),),
        (((0,), (0, 1, 2, 3)),),
    )
    firsts = (0, 0, 4, 6, 7)
    second = jnp.array([d for d, _ in kinds for _ in OFFSETS], jnp.int32)
    first = jnp.array([o for _ in kinds for o in OFFSETS], jnp.int32)
    other = jnp.array([w for _, w in kinds for _ in OFFSETS], jnp.int32)
    along_y = (core + other) % 2 == 0
    gx = (x - jnp.where(along_y, second, first) + 4) % 4
    gy = (y - jnp.where(along_y, first, second) + 4) % 4
    owners = (gx * 4 + gy % 2 * 2 + gy // 2) * 2 + other
    at_z = (z - jnp.array((0, 1, -1, 2), jnp.int32) + 4) % 4
    bases = ((((x * 4 + at_z) * 2 + yl) * 2 + yh) * 2 + core) * TILE
    steps = [steps_of(plan) for plan in plans]
    table = jnp.array([n for rows in steps for row in rows for n in row], jnp.int32)
    info = jnp.concatenate([bases, core[None], owners, table])

    def run(acc, call, rows, n_c=4, last=False):
        at_step = 5 + len(kinds) * PARTS + sum(4 * len(r) for r in steps[:call])
        at_owner = 5 + firsts[call] * PARTS
        return terms(acc, rows, classes[:n_c], plans[call], info, at_owner, at_step, last)

    own_swapped = swap(own)
    acc = run(None, 0, ((own,), (own_swapped,)), 3)
    c_far, acc, up = lax.optimization_barrier((c_far, acc, up))
    far = cross(up, 1, 1)
    classes = (c, c_up, c_down, c_far)
    acc = run(acc, 1, ((own,), (own_swapped,), (up,), (down,)))
    acc = run(acc, 2, ((swap(up),), (swap(down),)))
    acc, far = lax.optimization_barrier((acc, far))
    acc = run(acc, 3, ((far,),))
    sums = run(acc, 4, ((swap(far),),), last=True)
    parts = lax.all_to_all(sums, DEVICES, 0, 0, tiled=True)
    sums = jnp.sum(parts, axis=0)
    return margin_loss(sums[0], sums[1])


def margin_loss(other_sum, target_cos):
    sine = jnp.sqrt(jnp.maximum(1.0 - target_cos * target_cos, 0.0))
    shifted = target_cos * math.cos(MARGIN) - sine * math.sin(MARGIN)
    return jnp.log(other_sum + jnp.exp(LOGIT_SCALE * shifted)) - LOGIT_SCALE * shifted


def solution(mesh):
    finer = Mesh(mesh.devices.reshape(4, 4, 2, 2, 2), AXES)
    rows = ("yh", "c", "x", "z", "yl")
    placed = (P(rows, None), P(AXES, None), P(rows))
    return jax.shard_map(body, mesh=finer, in_specs=placed, out_specs=P(rows), check_vma=False)
```

```python
import functools
import math

import jax
import jax.numpy as jnp
from jax import lax
from jax.experimental import pallas as pl
from jax.experimental.pallas import tpu as pltpu
from jax.sharding import Mesh
from jax.sharding import PartitionSpec as P

AXES = ("x", "z", "yl", "yh", "c")
DEVICES = ("x", "yl", "yh", "c")
EPSILON = 1e-06
LOGIT_SCALE = 30.0
MARGIN = 0.5
SCALE2 = LOGIT_SCALE / math.log(2.0)
TILE = 512
WIDE = 1024
PARTS = 4
ROWS = 256
PITCH = 272
NT = (((1,), (1,)), ((), ()))
MIB = 1024 * 1024
OFFSETS = (0, 1, -1, 2)


def unit_block(ref):
    values = ref[...].astype(jnp.float32)
    total = jnp.sum(values * values, axis=1, keepdims=True)
    return (values * lax.rsqrt(total + EPSILON)).astype(jnp.bfloat16)


def unit_kernel(e_ref, c_ref, l_ref, a_ref, u_ref):
    u_ref[...] = unit_block(c_ref)
    rows = ROWS // 2
    here = pl.ds(pl.multiple_of(pl.program_id(0) * rows, rows), rows)
    a_ref[here, :] = unit_block(e_ref)
    label = jnp.concatenate([l_ref[...] // 256, l_ref[...] % 256], axis=1)
    label = jnp.broadcast_to(label.astype(jnp.float32), (PITCH - ROWS, 2 * ROWS))
    a_ref[ROWS:, :] = label.astype(jnp.bfloat16)


def normalized(embeddings, centers, labels):
    shapes = [(PITCH, embeddings.shape[1]), centers.shape]
    return pl.pallas_call(
        unit_kernel,
        grid=(2,),
        in_specs=[
            pl.BlockSpec((ROWS // 2, 512), lambda i: (i, 0)),
            pl.BlockSpec((TILE // 2, 512), lambda i: (i, 0)),
            pl.BlockSpec((1, ROWS), lambda i: (0, 0)),
        ],
        out_specs=[
            pl.BlockSpec((PITCH, 512), lambda i: (0, 0)),
            pl.BlockSpec((TILE // 2, 512), lambda i: (i, 0)),
        ],
        out_shape=[jax.ShapeDtypeStruct(s, jnp.bfloat16) for s in shapes],
    )(embeddings, centers, labels.reshape(1, ROWS))


def add_terms(x_ref, rel):
    ss, tt = [0.0, 0.0], [0.0, 0.0]
    for j in range(TILE // 8):
        x = x_ref[8 * j : 8 * j + 8, :]
        at_label = rel == 8 * j
        e = jnp.where(at_label, 0.0, jnp.exp2(x * SCALE2))
        i = j % 2
        ss[i] = ss[i] + e
        tt[i] = jnp.where(at_label, x, tt[i])
    return ss[0] + ss[1], tt[0] + tt[1]


def steps_of(plan):
    rows, seen_r, seen_k = [], set(), set()
    for tiles, pieces in plan:
        for r in tiles:
            for k in pieces:
                rows.append((r, k, int(r not in seen_r), int(k not in seen_k)))
                seen_r.add(r)
                seen_k.add(k)
    return rows


def terms_kernel(n_e, n_c, n_steps, at_owner, at_step, first, last, info_ref, *refs):
    refs = list(refs)
    if not first:
        refs.pop(0)
    e_refs = [refs.pop(0) for _ in range(n_e)]
    c_refs = [refs.pop(0) for _ in range(n_c)]
    acc_ref = refs.pop(0)
    out_ref = refs.pop(0) if last else None
    e_buf, l_buf, c_buf, even, odd, sems = refs

    def rows_copies(tile, ref):
        rows = e_buf.at[pl.ds(pl.multiple_of(tile * WIDE, WIDE), WIDE)]
        labels = ref.at[pl.ds(WIDE, PITCH - ROWS)]
        return [
            pltpu.make_async_copy(ref.at[pl.ds(0, WIDE)], rows, sems.at[tile]),
            pltpu.make_async_copy(labels, l_buf.at[tile], sems.at[n_e + tile]),
        ]

    def class_copy(k, ref):
        here = c_buf.at[pl.ds(pl.multiple_of(k * TILE, TILE), TILE)]
        return pltpu.make_async_copy(ref, here, sems.at[2 * n_e + k])

    def entry(step, which):
        return info_ref[at_step + 4 * step + which]

    starts = [[class_copy(k, ref)] for k, ref in enumerate(c_refs)]
    starts[1:1] = [rows_copies(0, e_refs[0])]
    starts += [rows_copies(r, e_refs[r]) for r in range(1, n_e)]
    for copies in starts:
        for copy in copies:
            copy.start()
    if first:
        acc_ref[...] = jnp.zeros_like(acc_ref)
    sub = lax.broadcasted_iota(jnp.int32, (8, WIDE), 0)

    def arrived(step):
        @pl.when(entry(step, 2) == 1)
        def _():
            for copy in rows_copies(entry(step, 0), e_refs[0]):
                copy.wait()

        @pl.when(entry(step, 3) == 1)
        def _():
            class_copy(entry(step, 1), c_refs[0]).wait()

    def product(step):
        rows = e_buf[pl.ds(pl.multiple_of(entry(step, 0) * WIDE, WIDE), WIDE), :]
        block = c_buf[pl.ds(pl.multiple_of(entry(step, 1) * TILE, TILE), TILE), :]
        return lax.dot_general(block, rows, NT, preferred_element_type=jnp.float32)

    def add(x_ref, step):
        n = entry(step, 0) * PARTS
        tile = l_buf[entry(step, 0)].astype(jnp.float32)
        parts = [tile[4 * i : 4 * i + 1].astype(jnp.int32) for i in range(PARTS)]
        lab = jnp.concatenate([h[:, :ROWS] * 256 + h[:, ROWS:] for h in parts], axis=1)
        s, t = add_terms(x_ref, lab - sub - info_ref[entry(step, 1)])
        for i in range(PARTS):
            o = info_ref[at_owner + n + i]
            acc_ref[o, 0:8, :] += s[:, ROWS * i : ROWS * i + ROWS]
            acc_ref[o, 8:16, :] += t[:, ROWS * i : ROWS * i + ROWS]

    arrived(0)
    even[...] = product(0)

    def two_steps(i, _):
        step = 2 * i
        more = step + 2 < n_steps
        arrived(step + 1)
        pl.when(more)(lambda: arrived(step + 2))
        odd[...] = product(step + 1)
        add(even, step)

        even[...] = product(jnp.minimum(step + 2, n_steps - 1))
        add(odd, step + 1)
        return 0

    lax.fori_loop(0, n_steps // 2, two_steps, 0)

    if last:
        core = info_ref[4]
        for o in range(32):
            for i in range(2):
                total = jnp.sum(acc_ref[o, 8 * i : 8 * i + 8, :], axis=0, keepdims=True)
                out_ref[o + core * (1 - 2 * (o % 2)), i : i + 1, :] = total


def terms(acc, tiles, classes, plan, info, at_owner, at_step, last=False):
    n_e, n_c, first = len(tiles), len(classes), acc is None
    rows = [piece for tile in tiles for piece in tile]
    smem = pl.BlockSpec(memory_space=pltpu.SMEM)
    vmem = pl.BlockSpec(memory_space=pltpu.VMEM)
    n_steps = len(steps_of(plan))
    sums = jax.ShapeDtypeStruct((32, 2, 256), jnp.float32)
    out = pl.pallas_call(
        functools.partial(terms_kernel, n_e, n_c, n_steps, at_owner, at_step, first, last),
        out_shape=[jax.ShapeDtypeStruct((32, 16, 256), jnp.float32)] + [sums] * last,
        in_specs=[smem] + [vmem] * (not first) + [pl.BlockSpec(memory_space=pl.ANY)] * (len(rows) + n_c),
        out_specs=[vmem] * (1 + last),
        scratch_shapes=[
            pltpu.VMEM((n_e * WIDE, 512), jnp.bfloat16),
            pltpu.VMEM((n_e, PITCH - ROWS, 512), jnp.bfloat16),
            pltpu.VMEM((n_c * TILE, 512), jnp.bfloat16),
            pltpu.VMEM((TILE, WIDE), jnp.float32),
            pltpu.VMEM((TILE, WIDE), jnp.float32),
            pltpu.SemaphoreType.DMA((2 * n_e + n_c,)),
        ],
        input_output_aliases={} if first else {1: 0},
        compiler_params=pltpu.CompilerParams(vmem_limit_bytes=24 * MIB),
        cost_estimate=pl.CostEstimate(
            flops=n_steps * 2 * TILE * WIDE * 512,
            bytes_accessed=(2 * n_e + n_c) * TILE * 1024,
            transcendentals=n_steps * TILE * WIDE,
        ),
    )(info, *([] if first else [acc]), *rows, *classes)
    return out[-1]


def cross(x, way, by):
    pairs = []
    for i in range(4):
        for y in range(4):
            for core in range(2):
                j, v = (i, (y + by) % 4) if core == way else ((i + by) % 4, y)
                pairs.append((place(i, y) * 2 + core, place(j, v) * 2 + core))
    return lax.ppermute(x, DEVICES, pairs)


def place(x, y):
    return x * 4 + y % 2 * 2 + y // 2


def swap(x):
    return lax.ppermute(x, "c", [(0, 1), (1, 0)])


def up_z(x, by):
    return lax.ppermute(x, "z", [(i, (i + by) % 4) for i in range(4)])


def body(embeddings, centers, labels):
    x, z, core = lax.axis_index("x"), lax.axis_index("z"), lax.axis_index("c")
    yl, yh = lax.axis_index("yl"), lax.axis_index("yh")
    y = yh * 2 + yl

    e, c = normalized(embeddings, centers, labels)
    c_up, c_down = up_z(c, 1), up_z(c, -1)
    e_up, e_down, e_far = cross(e, 0, 1), cross(e, 0, -1), cross(e, 0, 2)
    e_far, c_up, c_down, e_up, e_down = lax.optimization_barrier(
        (e_far, c_up, c_down, e_up, e_down)
    )
    parts = (e, e_up, e_down, e_far)
    below = [p[ROWS : ROWS + (PITCH - ROWS) // PARTS] for p in parts]
    own = jnp.concatenate([p[:ROWS] for p in parts] + below)
    up, down = cross(own, 1, 1), cross(own, 1, -1)
    c_far = up_z(c_up, 1)
    classes = (c, c_up, c_down, c_far)

    kinds = ((0, 0), (0, 1), (1, 0), (-1, 0), (1, 1), (-1, 1), (2, 0), (2, 1))
    plans = (
        (((0, 1), (0, 1, 2)),),
        (((2, 3), (0, 1, 2, 3)), ((0, 1), (3,))),
        (((0, 1), (0, 1, 2, 3)),),
        (((0,), (0, 1, 2, 3)),),
        (((0,), (0, 1, 2, 3)),),
    )
    firsts = (0, 0, 4, 6, 7)
    second = jnp.array([d for d, _ in kinds for _ in OFFSETS], jnp.int32)
    first = jnp.array([o for _ in kinds for o in OFFSETS], jnp.int32)
    other = jnp.array([w for _, w in kinds for _ in OFFSETS], jnp.int32)
    along_y = (core + other) % 2 == 0
    gx = (x - jnp.where(along_y, second, first) + 4) % 4
    gy = (y - jnp.where(along_y, first, second) + 4) % 4
    owners = (gx * 4 + gy % 2 * 2 + gy // 2) * 2 + other
    at_z = (z - jnp.array((0, 1, -1, 2), jnp.int32) + 4) % 4
    bases = ((((x * 4 + at_z) * 2 + yl) * 2 + yh) * 2 + core) * TILE
    steps = [steps_of(plan) for plan in plans]
    table = jnp.array([n for rows in steps for row in rows for n in row], jnp.int32)
    info = jnp.concatenate([bases, core[None], owners, table])

    def run(acc, call, rows, n_c=4, last=False):
        at_step = 5 + len(kinds) * PARTS + sum(4 * len(r) for r in steps[:call])
        at_owner = 5 + firsts[call] * PARTS
        return terms(acc, rows, classes[:n_c], plans[call], info, at_owner, at_step, last)

    own_swapped = swap(own)
    acc = run(None, 0, ((own,), (own_swapped,)), 3)
    acc, up = lax.optimization_barrier((acc, up))
    far = cross(up, 1, 1)
    down, c_far = lax.optimization_barrier((down, c_far))
    classes = (c, c_up, c_down, c_far)
    acc = run(acc, 1, ((own,), (own_swapped,), (up,), (down,)))
    acc = run(acc, 2, ((swap(up),), (swap(down),)))
    acc, far = lax.optimization_barrier((acc, far))
    acc = run(acc, 3, ((far,),))
    sums = run(acc, 4, ((swap(far),),), last=True)
    parts = lax.all_to_all(sums, DEVICES, 0, 0, tiled=True)
    sums = jnp.sum(parts, axis=0)
    return margin_loss(sums[0], sums[1])


def margin_loss(other_sum, target_cos):
    sine = jnp.sqrt(jnp.maximum(1.0 - target_cos * target_cos, 0.0))
    shifted = target_cos * math.cos(MARGIN) - sine * math.sin(MARGIN)
    return jnp.log(other_sum + jnp.exp(LOGIT_SCALE * shifted)) - LOGIT_SCALE * shifted


def solution(mesh):
    finer = Mesh(mesh.devices.reshape(4, 4, 2, 2, 2), AXES)
    rows = ("yh", "c", "x", "z", "yl")
    placed = (P(rows, None), P(AXES, None), P(rows))
    return jax.shard_map(body, mesh=finer, in_specs=placed, out_specs=P(rows), check_vma=False)
```
